32 devices in a mesh: groups: 2 (over x), sensor: 16 (over z, y, core).
Axes of the slice: x: 2, y: 2, z: 4, core: 2. Of those that a mesh axis runs over, the one named last changes fastest.
Arguments:
- series: bfloat16 [32, 32, 16384], P(None, None, ('groups', 'sensor')), parts along dimension 2, may hold values from -6 to 6
- caches: bfloat16 [2, 32, 2, 16384], P(None, None, None, ('groups', 'sensor')), parts along dimension 3, may hold values from -6 to 6
- dilation: int32 [2], replicated, may hold values from 1 to 2
- conv_weight: bfloat16 [2, 4, 32, 32], replicated, may hold values from -0.75 to 0.75
- conv_bias: float32 [2, 2, 32], replicated, may hold values from -3 to 3
- mix_weight: bfloat16 [2, 3, 32, 32], replicated, may hold values from -0.75 to 0.75
- mix_bias: float32 [2, 32], replicated, may hold values from -3 to 3
- skip_weight: bfloat16 [2, 256, 32], replicated, may hold values from -1 to 1
- block_cols: int32 [128, 5], P(('groups', 'sensor')), parts along dimension 0, may hold values from 0 to 63, as said below
- block_count: int32 [128], P(('groups', 'sensor')), parts along dimension 0, may hold values from 1 to 5, as said below
- edge_tiles: bfloat16 [128, 5, 128, 128], P(('groups', 'sensor')), parts along dimension 0, may hold values from -0.25 to 0.25
Outputs:
- next_series: bfloat16 [32, 32, 16384], P(None, None, ('groups', 'sensor')), parts along dimension 2
- skip_sum: bfloat16 [256, 8, 16384], P(None, None, ('groups', 'sensor')), parts along dimension 2
The draws below stay inside these ranges and needn't reach their ends.
There are 2 independent parts, one for each index of `groups`. The reference program is written for one: setup_inputs(seed, part) draws one part's arguments, and reference() takes and returns one part's arrays. A program takes and returns all parts, laid end to end along the dimension named above; an argument that names none is the same for every part. Nothing has to cross between parts.
Inputs may be any that keep to these rules, and one draw needn't show every extreme that they name: `block_cols`: slot s of row block r names block (r + o) mod 64 for some o with -2 <= o <= 2; the 5 slots of one row block name distinct blocks. Row block r uses its first block_count[r] slots; the other slots are ignored.
All inputs are finite; a program needn't handle non-finite values.
Results may differ from the reference program's by a relative error of at most 0.0057.
Values may be sent and summed in bfloat16 or wider, within the bound.
A program may use at most 64 MiB of HBM per device.

```python
import jax
import jax.numpy as jnp
from jax import lax

C = 32
SKIP = 256
BS = 128
TS = 32
LAYERS = 2
DMAX = 2
REACH = 2
SKT = 8
NNZ = 5
NB = 64
SENSORS = 8192


def draw_block_cols(key, part):
    subkeys = jax.random.split(key, NB)
    shuffled = jax.vmap(lambda single: jax.random.permutation(single, NNZ))(subkeys)
    row_index = jnp.arange(NB, dtype=jnp.int32)[:, None]
    return ((row_index + shuffled.astype(jnp.int32) - REACH) % NB).astype(jnp.int32)


def draw_block_count(key, part):
    counted = jax.random.randint(key, (NB,), 1, NNZ + 1, dtype=jnp.int32)
    position = jax.random.randint(jax.random.fold_in(key, 7), (), 0, NB, dtype=jnp.int32)
    return counted.at[position].set(NNZ).astype(jnp.int32)


def draw_dilation(key, part):
    roster = jax.random.randint(key, (LAYERS,), 1, DMAX + 1, dtype=jnp.int32)
    position = jax.random.randint(jax.random.fold_in(key, 11), (), 0, LAYERS, dtype=jnp.int32)
    roster = roster.at[position].set(DMAX)
    other = ((position + 1) % LAYERS).astype(jnp.int32)
    return roster.at[other].set(1).astype(jnp.int32)


def shard_levels(own_key, dims, pieces, smallest, largest):
    def one(dim, parts):
        steps = jax.random.uniform(jax.random.fold_in(jax.random.fold_in(own_key, 6), dim), (parts,), jnp.float32, smallest / len(pieces), largest / len(pieces))
        return jnp.repeat(jnp.exp(steps), dims[dim] // parts).reshape((-1,) + (1,) * (len(dims) - dim - 1))

    level = one(*pieces[0])
    for cut in pieces[1:]:
        level = level * one(*cut)
    return level


def normal_values(key, extent, deviation, most, shards=(), kind=jnp.bfloat16):
    entries = deviation * jax.random.normal(key, extent, jnp.float32)
    if shards:
        entries = entries * shard_levels(key, extent, shards, -0.22, 0.18)
    return jnp.clip(entries, -most, most).astype(kind)


def setup_inputs(seed: int = 0, part: int = 0) -> dict:
    streams_of = jax.random.split(jax.random.key(seed), 12)
    own_keys = jax.random.split(jax.random.fold_in(streams_of[11], part), 12)
    return {
        "series": normal_values(own_keys[0], (C, TS, SENSORS), 1.0, 6.0, ((2, 16),)),
        "caches": normal_values(own_keys[1], (LAYERS, C, DMAX, SENSORS), 1.0, 6.0, ((3, 16),)),
        "dilation": draw_dilation(jax.random.fold_in(streams_of[11], 71), part),
        "conv_weight": normal_values(streams_of[3], (LAYERS, 4, C, C), (2 * C) ** -0.5, 0.75),
        "conv_bias": normal_values(streams_of[4], (LAYERS, 2, C), 0.5, 3.0, (), jnp.float32),
        "mix_weight": normal_values(streams_of[5], (LAYERS, 3, C, C), (2 * C) ** -0.5, 0.75),
        "mix_bias": normal_values(streams_of[6], (LAYERS, C), 0.5, 3.0, (), jnp.float32),
        "skip_weight": normal_values(streams_of[7], (LAYERS, SKIP, C), C ** -0.5, 1.0),
        "block_cols": draw_block_cols(jax.random.fold_in(jax.random.fold_in(streams_of[11], part), 71), part),
        "block_count": draw_block_count(jax.random.fold_in(jax.random.fold_in(streams_of[11], part), 71), part),
        "edge_tiles": normal_values(own_keys[10], (NB, NNZ, BS, BS), (NNZ * BS) ** -0.5, 0.25, ((0, 16),)),
    }


def project(weight, field):
    rest = field.shape[1:]
    flat = field.reshape(field.shape[0], -1)
    product = jnp.dot(weight, flat, preferred_element_type=jnp.float32)
    return product.reshape((weight.shape[0],) + rest)


def diffuse(field, block_cols, block_count, edge_tiles):
    blocked = field.reshape(C, TS, NB, BS).astype(jnp.float32)
    accumulated = jnp.zeros((C, TS, NB, BS), jnp.float32)
    for slot_id in range(NNZ):
        live_rows = (block_count > slot_id).astype(jnp.float32)
        weights = edge_tiles[:, slot_id].astype(jnp.float32) * live_rows[:, None, None]
        picked = jnp.take(blocked, block_cols[:, slot_id], axis=2)
        accumulated = accumulated + jnp.einsum("ctrj,rij->ctri", picked, weights)
    return accumulated.reshape(C, TS, SENSORS)


def reference(series, caches, dilation, conv_weight, conv_bias, mix_weight, mix_bias, skip_weight, block_cols, block_count, edge_tiles):
    current = series
    skip_total = jnp.zeros((SKIP, SKT, SENSORS), jnp.float32)
    for layer_id in range(LAYERS):
        joined = jnp.concatenate([caches[layer_id], current], axis=1)
        begin = (DMAX - dilation[layer_id]).astype(jnp.int32)
        earlier = lax.dynamic_slice_in_dim(joined, begin, TS, 1)
        filter_value = project(conv_weight[layer_id, 0], earlier) + project(conv_weight[layer_id, 1], current) + conv_bias[layer_id, 0][:, None, None]
        gate_value = project(conv_weight[layer_id, 2], earlier) + project(conv_weight[layer_id, 3], current) + conv_bias[layer_id, 1][:, None, None]
        hidden = (jnp.tanh(filter_value) * jax.nn.sigmoid(gate_value)).astype(jnp.bfloat16)
        skip_total = skip_total + project(skip_weight[layer_id], hidden[:, TS - SKT:, :])
        first_hop = diffuse(hidden, block_cols, block_count, edge_tiles).astype(jnp.bfloat16)
        second_hop = diffuse(first_hop, block_cols, block_count, edge_tiles).astype(jnp.bfloat16)
        mixed = project(mix_weight[layer_id, 0], hidden) + project(mix_weight[layer_id, 1], first_hop) + project(mix_weight[layer_id, 2], second_hop) + mix_bias[layer_id][:, None, None]
        current = (current.astype(jnp.float32) + mixed).astype(jnp.bfloat16)
    return current, skip_total.astype(jnp.bfloat16)
```

```python
import functools

import jax
import jax.numpy as jnp
from jax import lax
from jax.experimental import pallas as pl
from jax.experimental.pallas import tpu as pltpu
from jax.sharding import PartitionSpec as P

LAYERS = 2
DMAX = 2
SKT = 8
LANES = 128
CHUNK = 8
GROUP = 4
HALF = 16
BF = jnp.bfloat16
F32 = jnp.float32


def dot(a, b):
    return jnp.dot(a, b, preferred_element_type=F32)


def iota(shape, dim):
    return lax.broadcasted_iota(jnp.int32, shape, dim)


def ones_where(mask):
    return jnp.where(mask, 1.0, 0.0).astype(BF)


def spread(weight, rows, columns):
    o, c = weight.shape
    tall = ones_where(iota((rows, o), 0) % o == iota((rows, o), 1))
    wide = ones_where(iota((c, columns), 1) % c == iota((c, columns), 0))
    return dot(tall, dot(weight, wide).astype(BF))


def column(row_vector, rows):
    c = row_vector.shape[1]
    mask = iota((rows, c), 0) % c == iota((rows, c), 1)
    return jnp.sum(jnp.where(mask, row_vector, 0.0), axis=1, keepdims=True)


def kernel(
    total_blocks,
    ring,
    series,
    caches,
    dilation,
    conv_weight,
    conv_bias,
    mix_weight,
    mix_bias,
    skip_weight,
    block_cols,
    block_count,
    edge_tiles,
    next_out,
    skip_out,
    ext,
    xbuf,
    ybuf,
    plan,
    conv_w,
    conv_b,
    mix_w,
    mix_b,
    skip_w,
    send_sem,
    recv_sem,
):
    channels, steps, width = series.shape
    blocks = width // LANES
    reach = (block_cols.shape[1] - 1) // 2
    pairs = blocks // 2
    rows = CHUNK * channels
    chunks = steps // CHUNK
    own = reach
    me = lax.axis_index("sensor")
    left, right = lax.rem(me + ring - 1, ring), lax.rem(me + 1, ring)

    barrier = pltpu.get_barrier_semaphore()
    for other in (left, right):
        pl.semaphore_signal(
            barrier, inc=1, device_id={"sensor": other}, device_id_type=pl.DeviceIdType.MESH
        )

    def halo(e, k):
        at = pl.ds(pl.multiple_of(k * rows, rows), rows)
        out = []
        for side, (target, source, landing) in enumerate(
            ((right, own + blocks - reach, 0), (left, own, own + blocks))
        ):
            out.append(
                pltpu.make_async_remote_copy(
                    src_ref=ext.at[e, pl.ds(source, reach), at, :],
                    dst_ref=ext.at[e, pl.ds(landing, reach), at, :],
                    send_sem=send_sem.at[e, k, side],
                    recv_sem=recv_sem.at[e, k, side],
                    device_id={"sensor": target},
                    device_id_type=pl.DeviceIdType.MESH,
                )
            )
        return out

    def build_conv(l):
        shape = (GROUP * channels, (GROUP + DMAX) * channels)
        to, ti = iota(shape, 0) // channels, iota(shape, 1) // channels
        late = ti == to + DMAX
        early = ti == to + DMAX - dilation[l]
        n = GROUP * channels
        for g in range(2):
            value = jnp.where(early, spread(conv_weight[l, 2 * g], *shape), 0.0) + jnp.where(
                late, spread(conv_weight[l, 2 * g + 1], *shape), 0.0
            )
            conv_w[l, pl.ds(g * n, n), :] = value.astype(BF)
            conv_b[l, pl.ds(g * n, n), :] = column(conv_bias[l, pl.ds(g, 1), :], n)

    def build_mix(l):
        diagonal = iota((rows, rows), 0) // channels == iota((rows, rows), 1) // channels
        for j in range(3):
            value = jnp.where(diagonal, spread(mix_weight[l, j], rows, rows), 0.0)
            mix_w[l, j] = value.astype(BF)
        mix_b[l] = column(mix_bias[pl.ds(l, 1), :], rows)

    def build_skip(l):
        o, c = skip_weight.shape[1:]
        piece = 512
        wide = ones_where(iota((c, SKT * c), 1) % c == iota((c, SKT * c), 0))
        repeated = dot(skip_weight[l], wide).astype(BF)

        def step(i, carry):
            tall = ones_where(
                iota((piece, o), 0) // SKT + i * (piece // SKT) == iota((piece, o), 1)
            )
            mask = iota((piece, SKT * c), 0) % SKT == iota((piece, SKT * c), 1) // c
            at = pl.ds(pl.multiple_of(i * piece, piece), piece)
            skip_w[l, at, :] = jnp.where(mask, dot(tall, repeated), 0.0).astype(BF)
            return carry

        lax.fori_loop(0, o * SKT // piece, step, 0)

    def build_plan():
        plan[...] = jnp.zeros_like(plan)
        nonzero = block_cols.shape[1]
        for r in range(blocks):
            row = me * blocks + r
            where = [
                lax.rem(block_cols[r, s] - row + reach + total_blocks, total_blocks)
                for s in range(nonzero)
            ]
            for o in range(nonzero):
                value = jnp.zeros((LANES, LANES), F32)
                for s in range(nonzero):
                    live = jnp.logical_and(where[s] == o, block_count[r] > s)
                    scale = jnp.where(live, 1.0, 0.0).astype(F32)
                    value = value + scale * edge_tiles[r, s].astype(F32)
                plan[
                    r // 2,
                    pl.ds((r % 2 + o) * LANES, LANES),
                    pl.ds((r % 2) * LANES, LANES),
                ] = value.T.astype(BF)

    def gated(l, e, k):
        n = GROUP * channels
        for g in range(CHUNK // GROUP):
            start = pl.multiple_of(k * rows + g * n, n)
            for q in range(pairs):
                cols = pl.ds(q * 2 * LANES, 2 * LANES)
                x = xbuf[l, pl.ds(start, (GROUP + DMAX) * channels), cols]
                both = dot(conv_w[l], x) + conv_b[l]
                gate = 0.5 * jnp.tanh(0.5 * both[n:]) + 0.5
                hidden = (jnp.tanh(both[:n]) * gate).astype(BF)
                ext[e, own + 2 * q, pl.ds(start, n), :] = hidden[:, :LANES]
                ext[e, own + 2 * q + 1, pl.ds(start, n), :] = hidden[:, LANES:]

    def diffused(e, k, q):
        at = pl.ds(pl.multiple_of(k * rows, rows), rows)
        source = jnp.concatenate(
            [ext[e, 2 * q + j, at, :] for j in range(2 * reach + 2)], axis=1
        )
        return dot(source, plan[q]).astype(BF)

    def first(e, k):
        at = pl.ds(pl.multiple_of(k * rows, rows), rows)
        for q in range(pairs):
            value = diffused(e, k, q)
            ext[e + 1, own + 2 * q, at, :] = value[:, :LANES]
            ext[e + 1, own + 2 * q + 1, at, :] = value[:, LANES:]

    def pair_of(e, k, q):
        at = pl.ds(pl.multiple_of(k * rows, rows), rows)
        return jnp.concatenate(
            [ext[e, own + 2 * q, at, :], ext[e, own + 2 * q + 1, at, :]], axis=1
        )

    def mixed(l, e, k, q):
        cols = pl.ds(q * 2 * LANES, 2 * LANES)
        second = diffused(e + 1, k, q)
        value = (
            dot(mix_w[l, 0], pair_of(e, k, q))
            + dot(mix_w[l, 1], pair_of(e + 1, k, q))
            + dot(mix_w[l, 2], second)
            + mix_b[l]
        )
        at = pl.ds(pl.multiple_of(k * rows + DMAX * channels, channels), rows)
        return (xbuf[l, at, cols].astype(F32) + value).astype(BF)

    def start_halo(e, k):
        for copy in halo(e, k):
            copy.start()

    def wait_halo(e, k):
        for copy in halo(e, k):
            copy.wait_recv()

    def each(body):
        def step(k, carry):
            body(k)
            return carry

        lax.fori_loop(0, chunks, step, 0)

    half_rows = HALF * channels
    square = (half_rows, half_rows)
    for l in range(LAYERS):
        xbuf[l, pl.ds(0, DMAX * channels), :] = caches[l]
    build_conv(0)
    i0, i1 = iota(square, 0), iota(square, 1)
    forward = ones_where((i0 % channels) * HALF + i0 // channels == i1)
    for h in range(steps // HALF):
        piece = series[:, pl.ds(h * HALF, HALF), :].reshape(half_rows, width)
        xbuf[0, pl.ds(DMAX * channels + h * half_rows, half_rows), :] = dot(
            forward, piece
        ).astype(BF)

    pl.semaphore_wait(barrier, 2)

    def hidden_zero(k):
        gated(0, 0, k)
        start_halo(0, k)

    each(hidden_zero)
    build_plan()
    build_conv(1)
    build_mix(0)

    def first_zero(k):
        wait_halo(0, k)
        first(0, k)
        start_halo(1, k)

    each(first_zero)
    build_mix(1)
    build_skip(0)

    def second_zero(k):
        wait_halo(1, k)
        at = pl.ds(pl.multiple_of(k * rows + DMAX * channels, channels), rows)
        for q in range(pairs):
            xbuf[1, at, pl.ds(q * 2 * LANES, 2 * LANES)] = mixed(0, 0, k, q)
        gated(1, 2, k)
        start_halo(2, k)

    each(second_zero)
    build_skip(1)

    def first_one(k):
        wait_halo(2, k)
        first(2, k)
        start_halo(3, k)

    each(first_one)

    piece = 256
    count = skip_out.shape[0] // piece

    def skip_step(i, carry):
        at = pl.ds(pl.multiple_of(i * piece, piece), piece)
        for q in range(pairs):
            value = dot(skip_w[0, at, :], pair_of(0, chunks - 1, q)) + dot(
                skip_w[1, at, :], pair_of(2, chunks - 1, q)
            )
            skip_out[at, pl.ds(q * 2 * LANES, 2 * LANES)] = value.astype(BF)
        return carry

    lax.fori_loop(0, count, skip_step, 0)

    def second_one(k):
        wait_halo(3, k)
        at = pl.ds(pl.multiple_of(k * rows, rows), rows)
        for q in range(pairs):
            ybuf[at, pl.ds(q * 2 * LANES, 2 * LANES)] = mixed(1, 2, k, q)

    each(second_one)
    backward = ones_where((i0 % HALF) * channels + i0 // HALF == i1)
    for h in range(steps // HALF):
        value = dot(backward, ybuf[pl.ds(h * half_rows, half_rows), :]).astype(BF)
        next_out[:, pl.ds(h * HALF, HALF), :] = value.reshape(channels, HALF, width)

    for e in range(2 * LAYERS):

        def drain(k, e=e):
            for copy in halo(e, k):
                copy.wait_send()

        each(drain)


def on_device(
    series,
    caches,
    dilation,
    conv_weight,
    conv_bias,
    mix_weight,
    mix_bias,
    skip_weight,
    block_cols,
    block_count,
    edge_tiles,
):
    channels, steps, width = series.shape
    blocks, nonzero = block_cols.shape
    ring = lax.axis_size("sensor")
    reach = (nonzero - 1) // 2
    skips = skip_weight.shape[1]
    rows = CHUNK * channels
    chunks = steps // CHUNK
    caches = caches.transpose(0, 2, 1, 3).reshape(LAYERS, DMAX * channels, width)
    vmem, smem = pl.BlockSpec(memory_space=pltpu.VMEM), pl.BlockSpec(memory_space=pltpu.SMEM)
    following, skip = pl.pallas_call(
        functools.partial(kernel, blocks * ring, ring),
        out_shape=(
            jax.ShapeDtypeStruct((channels, steps, width), BF),
            jax.ShapeDtypeStruct((skips * SKT, width), BF),
        ),
        in_specs=[vmem, vmem, smem, vmem, vmem, vmem, vmem, vmem, smem, smem, vmem],
        out_specs=(vmem, vmem),
        scratch_shapes=[
            pltpu.VMEM((2 * LAYERS, blocks + 2 * reach, steps * channels, LANES), BF),
            pltpu.VMEM((LAYERS, (steps + DMAX) * channels, width), BF),
            pltpu.VMEM((steps * channels, width), BF),
            pltpu.VMEM((blocks // 2, (nonzero + 1) * LANES, 2 * LANES), BF),
            pltpu.VMEM((LAYERS, 2 * GROUP * channels, (GROUP + DMAX) * channels), BF),
            pltpu.VMEM((LAYERS, 2 * GROUP * channels, 1), F32),
            pltpu.VMEM((LAYERS, 3, rows, rows), BF),
            pltpu.VMEM((LAYERS, rows, 1), F32),
            pltpu.VMEM((LAYERS, skips * SKT, SKT * channels), BF),
            pltpu.SemaphoreType.DMA((2 * LAYERS, chunks, 2)),
            pltpu.SemaphoreType.DMA((2 * LAYERS, chunks, 2)),
        ],
        compiler_params=pltpu.CompilerParams(
            collective_id=0, has_side_effects=True, vmem_limit_bytes=48 * 2**20
        ),
    )(
        series,
        caches,
        dilation,
        conv_weight,
        conv_bias,
        mix_weight,
        mix_bias,
        skip_weight,
        block_cols,
        block_count,
        edge_tiles,
    )
    return following, skip.reshape(skips, SKT, width)


def solution(mesh):
    in_specs = (
        P(None, None, ("groups", "sensor")),
        P(None, None, None, ("groups", "sensor")),
        P(),
        P(),
        P(),
        P(),
        P(),
        P(),
        P(("groups", "sensor"), None),
        P(("groups", "sensor")),
        P(("groups", "sensor"), None, None, None),
    )
    out_specs = (P(None, None, ("groups", "sensor")), P(None, None, ("groups", "sensor")))
    return jax.shard_map(
        on_device, mesh=mesh, in_specs=in_specs, out_specs=out_specs, check_vma=False
    )
```

```python
import functools

import jax
import jax.numpy as jnp
from jax import lax
from jax.experimental import pallas as pl
from jax.experimental.pallas import tpu as pltpu
from jax.sharding import PartitionSpec as P

LAYERS = 2
DMAX = 2
SKT = 8
LANES = 128
CHUNK = 8
GROUP = 4
HALF = 16
BF = jnp.bfloat16
F32 = jnp.float32


def dot(a, b):
    return jnp.dot(a, b, preferred_element_type=F32)


def iota(shape, dim):
    return lax.broadcasted_iota(jnp.int32, shape, dim)


def ones_where(mask):
    return jnp.where(mask, 1.0, 0.0).astype(BF)


def spread(weight, rows, columns):
    o, c = weight.shape
    tall = ones_where(iota((rows, o), 0) % o == iota((rows, o), 1))
    wide = ones_where(iota((c, columns), 1) % c == iota((c, columns), 0))
    return dot(tall, dot(weight, wide).astype(BF))


def column(row_vector, rows):
    c = row_vector.shape[1]
    mask = iota((rows, c), 0) % c == iota((rows, c), 1)
    return jnp.sum(jnp.where(mask, row_vector, 0.0), axis=1, keepdims=True)


def kernel(
    total_blocks,
    ring,
    series_in,
    caches_in,
    dilation_in,
    conv_weight_in,
    conv_bias_in,
    mix_weight_in,
    mix_bias_in,
    skip_weight_in,
    block_cols_in,
    block_count_in,
    edge_tiles_in,
    next_hbm,
    skip_hbm,
    next_out,
    skip_out,
    ext,
    xbuf,
    ybuf,
    plan,
    conv_w,
    conv_b,
    mix_w,
    mix_b,
    skip_w,
    send_sem,
    recv_sem,
    load_sem,
    store_sem,
    series,
    caches,
    dilation,
    conv_weight,
    conv_bias,
    mix_weight,
    mix_bias,
    skip_weight,
    block_cols,
    block_count,
    edge_tiles,
):
    channels, steps, width = series.shape
    blocks = width // LANES
    reach = (block_cols.shape[1] - 1) // 2
    pairs = blocks // 2
    rows = CHUNK * channels
    chunks = steps // CHUNK
    own = reach
    me = lax.axis_index("sensor")
    left, right = lax.rem(me + ring - 1, ring), lax.rem(me + 1, ring)

    halves = steps // HALF
    loads = [
        pltpu.make_async_copy(
            series_in.at[:, pl.ds(h * HALF, HALF), :],
            series.at[:, pl.ds(h * HALF, HALF), :],
            load_sem.at[h],
        )
        for h in range(halves)
    ]
    for source, target in (
        (conv_weight_in, conv_weight),
        (conv_bias_in, conv_bias),
        (dilation_in, dilation),
        (caches_in, caches),
        (edge_tiles_in, edge_tiles),
        (block_cols_in, block_cols),
        (block_count_in, block_count),
        (mix_weight_in, mix_weight),
        (mix_bias_in, mix_bias),
        (skip_weight_in, skip_weight),
    ):
        loads.append(pltpu.make_async_copy(source, target, load_sem.at[len(loads)]))
    for load in loads:
        load.start()

    barrier = pltpu.get_barrier_semaphore()
    for other in (left, right):
        pl.semaphore_signal(
            barrier, inc=1, device_id={"sensor": other}, device_id_type=pl.DeviceIdType.MESH
        )

    def halo(e, k):
        at = pl.ds(pl.multiple_of(k * rows, rows), rows)
        out = []
        for side, (target, source, landing) in enumerate(
            ((right, own + blocks - reach, 0), (left, own, own + blocks))
        ):
            out.append(
                pltpu.make_async_remote_copy(
                    src_ref=ext.at[e, pl.ds(source, reach), at, :],
                    dst_ref=ext.at[e, pl.ds(landing, reach), at, :],
                    send_sem=send_sem.at[e, k, side],
                    recv_sem=recv_sem.at[e, k, side],
                    device_id={"sensor": target},
                    device_id_type=pl.DeviceIdType.MESH,
                )
            )
        return out

    def build_conv(l):
        shape = (GROUP * channels, (GROUP + DMAX) * channels)
        to, ti = iota(shape, 0) // channels, iota(shape, 1) // channels
        late = ti == to + DMAX
        early = ti == to + DMAX - dilation[l]
        n = GROUP * channels
        for g in range(2):
            value = jnp.where(early, spread(conv_weight[l, 2 * g], *shape), 0.0) + jnp.where(
                late, spread(conv_weight[l, 2 * g + 1], *shape), 0.0
            )
            conv_w[l, pl.ds(g * n, n), :] = value.astype(BF)
            conv_b[l, pl.ds(g * n, n), :] = column(conv_bias[l, pl.ds(g, 1), :], n)

    def build_mix(l):
        diagonal = iota((rows, rows), 0) // channels == iota((rows, rows), 1) // channels
        for j in range(3):
            value = jnp.where(diagonal, spread(mix_weight[l, j], rows, rows), 0.0)
            mix_w[l, j] = value.astype(BF)
        mix_b[l] = column(mix_bias[pl.ds(l, 1), :], rows)

    def build_skip(l):
        c, o = skip_weight.shape[1:]
        piece = 512
        wide = ones_where(iota((c, SKT * c), 1) % c == iota((c, SKT * c), 0))
        repeated = dot(skip_weight[l].astype(F32).T.astype(BF), wide).astype(BF)

        def step(i, carry):
            tall = ones_where(
                iota((piece, o), 0) // SKT + i * (piece // SKT) == iota((piece, o), 1)
            )
            mask = iota((piece, SKT * c), 0) % SKT == iota((piece, SKT * c), 1) // c
            at = pl.ds(pl.multiple_of(i * piece, piece), piece)
            skip_w[l, at, :] = jnp.where(mask, dot(tall, repeated), 0.0).astype(BF)
            return carry

        lax.fori_loop(0, o * SKT // piece, step, 0)

    def build_plan():
        plan[...] = jnp.zeros_like(plan)
        nonzero = block_cols.shape[1]
        for r in range(blocks):
            row = me * blocks + r
            where = [
                lax.rem(block_cols[r, s] - row + reach + total_blocks, total_blocks)
                for s in range(nonzero)
            ]
            for o in range(nonzero):
                value = jnp.zeros((LANES, LANES), F32)
                for s in range(nonzero):
                    live = jnp.logical_and(where[s] == o, block_count[r] > s)
                    scale = jnp.where(live, 1.0, 0.0).astype(F32)
                    value = value + scale * edge_tiles[r, s].astype(F32)
                plan[
                    r // 2,
                    pl.ds((r % 2 + o) * LANES, LANES),
                    pl.ds((r % 2) * LANES, LANES),
                ] = value.T.astype(BF)

    def gated(l, e, k):
        n = GROUP * channels
        for g in range(CHUNK // GROUP):
            start = pl.multiple_of(k * rows + g * n, n)
            for q in range(pairs):
                cols = pl.ds(q * 2 * LANES, 2 * LANES)
                x = xbuf[l, pl.ds(start, (GROUP + DMAX) * channels), cols]
                both = dot(conv_w[l], x) + conv_b[l]
                gate = 0.5 * jnp.tanh(0.5 * both[n:]) + 0.5
                hidden = (jnp.tanh(both[:n]) * gate).astype(BF)
                ext[e, own + 2 * q, pl.ds(start, n), :] = hidden[:, :LANES]
                ext[e, own + 2 * q + 1, pl.ds(start, n), :] = hidden[:, LANES:]

    def diffused(e, k, q):
        at = pl.ds(pl.multiple_of(k * rows, rows), rows)
        source = jnp.concatenate(
            [ext[e, 2 * q + j, at, :] for j in range(2 * reach + 2)], axis=1
        )
        return dot(source, plan[q]).astype(BF)

    def first(e, k):
        at = pl.ds(pl.multiple_of(k * rows, rows), rows)
        for q in range(pairs):
            value = diffused(e, k, q)
            ext[e + 1, own + 2 * q, at, :] = value[:, :LANES]
            ext[e + 1, own + 2 * q + 1, at, :] = value[:, LANES:]

    def pair_of(e, k, q):
        at = pl.ds(pl.multiple_of(k * rows, rows), rows)
        return jnp.concatenate(
            [ext[e, own + 2 * q, at, :], ext[e, own + 2 * q + 1, at, :]], axis=1
        )

    def mixed(l, e, k, q):
        cols = pl.ds(q * 2 * LANES, 2 * LANES)
        second = diffused(e + 1, k, q)
        value = (
            dot(mix_w[l, 0], pair_of(e, k, q))
            + dot(mix_w[l, 1], pair_of(e + 1, k, q))
            + dot(mix_w[l, 2], second)
            + mix_b[l]
        )
        at = pl.ds(pl.multiple_of(k * rows + DMAX * channels, channels), rows)
        return (xbuf[l, at, cols].astype(F32) + value).astype(BF)

    def start_halo(e, k):
        for copy in halo(e, k):
            copy.start()

    def wait_halo(e, k):
        for copy in halo(e, k):
            copy.wait_recv()

    def each(body):
        def step(k, carry):
            body(k)
            return carry

        lax.fori_loop(0, chunks, step, 0)

    def each_half(h, step):
        per = HALF // CHUNK
        lax.fori_loop(h * per, (h + 1) * per, step, 0)

    half_rows = HALF * channels
    square = (half_rows, half_rows)
    i0, i1 = iota(square, 0), iota(square, 1)
    forward = ones_where((i0 % channels) * HALF + i0 // channels == i1)
    for load in loads[halves : halves + 4]:
        load.wait()
    build_conv(0)
    for l in range(LAYERS):
        xbuf[l, pl.ds(0, DMAX * channels), :] = caches[l]

    def hidden_zero(k, carry):
        gated(0, 0, k)
        start_halo(0, k)
        return carry

    for h in range(halves):
        loads[h].wait()
        piece = series[:, pl.ds(h * HALF, HALF), :].reshape(half_rows, width)
        xbuf[0, pl.ds(DMAX * channels + h * half_rows, half_rows), :] = dot(
            forward, piece
        ).astype(BF)
        if h == 0:
            pl.semaphore_wait(barrier, 2)
        each_half(h, hidden_zero)
    for load in loads[halves + 4 :]:
        load.wait()
    build_plan()
    build_conv(1)
    build_mix(0)

    def first_zero(k):
        wait_halo(0, k)
        first(0, k)
        start_halo(1, k)

    each(first_zero)
    build_mix(1)
    build_skip(0)

    def second_zero(k):
        wait_halo(1, k)
        at = pl.ds(pl.multiple_of(k * rows + DMAX * channels, channels), rows)
        for q in range(pairs):
            xbuf[1, at, pl.ds(q * 2 * LANES, 2 * LANES)] = mixed(0, 0, k, q)
        gated(1, 2, k)
        start_halo(2, k)

    each(second_zero)
    build_skip(1)

    def first_one(k):
        wait_halo(2, k)
        first(2, k)
        start_halo(3, k)

    each(first_one)

    piece = 256
    count = skip_out.shape[0] // piece

    def skip_step(i, carry):
        at = pl.ds(pl.multiple_of(i * piece, piece), piece)
        for q in range(pairs):
            value = dot(skip_w[0, at, :], pair_of(0, chunks - 1, q)) + dot(
                skip_w[1, at, :], pair_of(2, chunks - 1, q)
            )
            skip_out[at, pl.ds(q * 2 * LANES, 2 * LANES)] = value.astype(BF)
        return carry

    lax.fori_loop(0, count, skip_step, 0)
    stores = [pltpu.make_async_copy(skip_out, skip_hbm, store_sem.at[halves])]
    stores[0].start()

    backward = ones_where((i0 % HALF) * channels + i0 // HALF == i1)

    def second_one(k, carry):
        wait_halo(3, k)
        at = pl.ds(pl.multiple_of(k * rows, rows), rows)
        for q in range(pairs):
            ybuf[at, pl.ds(q * 2 * LANES, 2 * LANES)] = mixed(1, 2, k, q)
        return carry

    for h in range(halves):
        each_half(h, second_one)
        value = dot(backward, ybuf[pl.ds(h * half_rows, half_rows), :]).astype(BF)
        next_out[:, pl.ds(h * HALF, HALF), :] = value.reshape(channels, HALF, width)
        stores.append(
            pltpu.make_async_copy(
                next_out.at[:, pl.ds(h * HALF, HALF), :],
                next_hbm.at[:, pl.ds(h * HALF, HALF), :],
                store_sem.at[h],
            )
        )
        stores[-1].start()

    for e in range(2 * LAYERS):

        def drain(k, e=e):
            for copy in halo(e, k):
                copy.wait_send()

        each(drain)
    for store in stores:
        store.wait()


def on_device(
    series,
    caches,
    dilation,
    conv_weight,
    conv_bias,
    mix_weight,
    mix_bias,
    skip_weight,
    block_cols,
    block_count,
    edge_tiles,
):
    channels, steps, width = series.shape
    blocks, nonzero = block_cols.shape
    ring = lax.axis_size("sensor")
    reach = (nonzero - 1) // 2
    skips = skip_weight.shape[1]
    rows = CHUNK * channels
    chunks = steps // CHUNK
    caches = caches.transpose(0, 2, 1, 3).reshape(LAYERS, DMAX * channels, width)
    skip_weight = skip_weight.transpose(0, 2, 1)
    hbm = pl.BlockSpec(memory_space=pltpu.HBM)
    operands = (
        series,
        caches,
        dilation,
        conv_weight,
        conv_bias,
        mix_weight,
        mix_bias,
        skip_weight,
        block_cols,
        block_count,
        edge_tiles,
    )
    small = (2, 8, 9)
    places = [
        (pltpu.SMEM if i in small else pltpu.VMEM)(x.shape, x.dtype)
        for i, x in enumerate(operands)
    ]
    loads = len(operands) - 1 + steps // HALF
    following, skip = pl.pallas_call(
        functools.partial(kernel, blocks * ring, ring),
        out_shape=(
            jax.ShapeDtypeStruct((channels, steps, width), BF),
            jax.ShapeDtypeStruct((skips * SKT, width), BF),
        ),
        in_specs=[hbm] * len(operands),
        out_specs=(hbm, hbm),
        scratch_shapes=[
            pltpu.VMEM((channels, steps, width), BF),
            pltpu.VMEM((skips * SKT, width), BF),
            pltpu.VMEM((2 * LAYERS, blocks + 2 * reach, steps * channels, LANES), BF),
            pltpu.VMEM((LAYERS, (steps + DMAX) * channels, width), BF),
            pltpu.VMEM((steps * channels, width), BF),
            pltpu.VMEM((blocks // 2, (nonzero + 1) * LANES, 2 * LANES), BF),
            pltpu.VMEM((LAYERS, 2 * GROUP * channels, (GROUP + DMAX) * channels), BF),
            pltpu.VMEM((LAYERS, 2 * GROUP * channels, 1), F32),
            pltpu.VMEM((LAYERS, 3, rows, rows), BF),
            pltpu.VMEM((LAYERS, rows, 1), F32),
            pltpu.VMEM((LAYERS, skips * SKT, SKT * channels), BF),
            pltpu.SemaphoreType.DMA((2 * LAYERS, chunks, 2)),
            pltpu.SemaphoreType.DMA((2 * LAYERS, chunks, 2)),
            pltpu.SemaphoreType.DMA((loads,)),
            pltpu.SemaphoreType.DMA((steps // HALF + 1,)),
            *places,
        ],
        compiler_params=pltpu.CompilerParams(
            collective_id=0, has_side_effects=True, vmem_limit_bytes=60 * 2**20
        ),
    )(*operands)
    return following, skip.reshape(skips, SKT, width)


def solution(mesh):
    in_specs = (
        P(None, None, ("groups", "sensor")),
        P(None, None, None, ("groups", "sensor")),
        P(),
        P(),
        P(),
        P(),
        P(),
        P(),
        P(("groups", "sensor"), None),
        P(("groups", "sensor")),
        P(("groups", "sensor"), None, None, None),
    )
    out_specs = (P(None, None, ("groups", "sensor")), P(None, None, ("groups", "sensor")))
    return jax.shard_map(
        on_device, mesh=mesh, in_specs=in_specs, out_specs=out_specs, check_vma=False
    )
```

```python
import functools

import jax
import jax.numpy as jnp
from jax import lax
from jax.experimental import pallas as pl
from jax.experimental.pallas import tpu as pltpu
from jax.sharding import PartitionSpec as P

LAYERS = 2
DMAX = 2
SKT = 8
LANES = 128
CHUNK = 8
GROUP = 4
HALF = 16
BF = jnp.bfloat16
F32 = jnp.float32


def dot(a, b):
    return jnp.dot(a, b, preferred_element_type=F32)


def iota(shape, dim):
    return lax.broadcasted_iota(jnp.int32, shape, dim)


def ones_where(mask):
    return jnp.where(mask, 1.0, 0.0).astype(BF)


def spread(weight, rows, columns):
    o, c = weight.shape
    tall = ones_where(iota((rows, o), 0) % o == iota((rows, o), 1))
    wide = ones_where(iota((c, columns), 1) % c == iota((c, columns), 0))
    return dot(tall, dot(weight, wide).astype(BF))


def column(row_vector, rows):
    c = row_vector.shape[1]
    mask = iota((rows, c), 0) % c == iota((rows, c), 1)
    return jnp.sum(jnp.where(mask, row_vector, 0.0), axis=1, keepdims=True)


def kernel(
    total_blocks,
    ring,
    series_in,
    caches_in,
    dilation_in,
    conv_weight_in,
    conv_bias_in,
    mix_weight_in,
    mix_bias_in,
    skip_weight_in,
    block_cols_in,
    block_count_in,
    edge_tiles_in,
    next_hbm,
    skip_hbm,
    skip_out,
    ext,
    xbuf,
    ybuf,
    plan,
    conv_w,
    conv_b,
    mix_w,
    mix_b,
    skip_w,
    send_sem,
    recv_sem,
    load_sem,
    store_sem,
    series,
    caches,
    dilation,
    conv_weight,
    conv_bias,
    mix_weight,
    mix_bias,
    skip_weight,
    block_cols,
    block_count,
    edge_tiles,
):
    channels, steps, width = series.shape
    blocks = width // LANES
    reach = (block_cols.shape[1] - 1) // 2
    pairs = blocks // 2
    rows = CHUNK * channels
    chunks = steps // CHUNK
    own = reach
    me = lax.axis_index("sensor")
    left, right = lax.rem(me + ring - 1, ring), lax.rem(me + 1, ring)

    halves = steps // HALF
    loads = [
        pltpu.make_async_copy(
            series_in.at[:, pl.ds(h * HALF, HALF), :],
            series.at[:, pl.ds(h * HALF, HALF), :],
            load_sem.at[h],
        )
        for h in range(halves)
    ]
    for source, target in (
        (conv_weight_in, conv_weight),
        (conv_bias_in, conv_bias),
        (dilation_in, dilation),
        (caches_in, caches),
        (edge_tiles_in, edge_tiles),
        (block_cols_in, block_cols),
        (block_count_in, block_count),
        (mix_weight_in, mix_weight),
        (mix_bias_in, mix_bias),
        (skip_weight_in, skip_weight),
    ):
        loads.append(pltpu.make_async_copy(source, target, load_sem.at[len(loads)]))
    for load in loads:
        load.start()

    barrier = pltpu.get_barrier_semaphore()
    for other in (left, right):
        pl.semaphore_signal(
            barrier, inc=1, device_id={"sensor": other}, device_id_type=pl.DeviceIdType.MESH
        )

    def halo(e, k):
        at = pl.ds(pl.multiple_of(k * rows, rows), rows)
        out = []
        for side, (target, source, landing) in enumerate(
            ((right, own + blocks - reach, 0), (left, own, own + blocks))
        ):
            out.append(
                pltpu.make_async_remote_copy(
                    src_ref=ext.at[e, pl.ds(source, reach), at, :],
                    dst_ref=ext.at[e, pl.ds(landing, reach), at, :],
                    send_sem=send_sem.at[e, k, side],
                    recv_sem=recv_sem.at[e, k, side],
                    device_id={"sensor": target},
                    device_id_type=pl.DeviceIdType.MESH,
                )
            )
        return out

    def build_conv(l):
        shape = (GROUP * channels, (GROUP + DMAX) * channels)
        to, ti = iota(shape, 0) // channels, iota(shape, 1) // channels
        late = ti == to + DMAX
        early = ti == to + DMAX - dilation[l]
        n = GROUP * channels
        for g in range(2):
            value = jnp.where(early, spread(conv_weight[l, 2 * g], *shape), 0.0) + jnp.where(
                late, spread(conv_weight[l, 2 * g + 1], *shape), 0.0
            )
            conv_w[l, pl.ds(g * n, n), :] = value.astype(BF)
            conv_b[l, pl.ds(g * n, n), :] = column(conv_bias[l, pl.ds(g, 1), :], n)

    def build_mix(l):
        diagonal = iota((rows, rows), 0) // channels == iota((rows, rows), 1) // channels
        for j in range(3):
            value = jnp.where(diagonal, spread(mix_weight[l, j], rows, rows), 0.0)
            mix_w[l, j] = value.astype(BF)
        mix_b[l] = column(mix_bias[pl.ds(l, 1), :], rows)

    def build_skip(l):
        c, o = skip_weight.shape[1:]
        piece = 512
        wide = ones_where(iota((c, SKT * c), 1) % c == iota((c, SKT * c), 0))
        repeated = dot(skip_weight[l].astype(F32).T.astype(BF), wide).astype(BF)

        def step(i, carry):
            tall = ones_where(
                iota((piece, o), 0) // SKT + i * (piece // SKT) == iota((piece, o), 1)
            )
            mask = iota((piece, SKT * c), 0) % SKT == iota((piece, SKT * c), 1) // c
            at = pl.ds(pl.multiple_of(i * piece, piece), piece)
            skip_w[l, at, :] = jnp.where(mask, dot(tall, repeated), 0.0).astype(BF)
            return carry

        lax.fori_loop(0, o * SKT // piece, step, 0)

    def build_plan():
        plan[...] = jnp.zeros_like(plan)
        nonzero = block_cols.shape[1]
        for r in range(blocks):
            row = me * blocks + r
            where = [
                lax.rem(block_cols[r, s] - row + reach + total_blocks, total_blocks)
                for s in range(nonzero)
            ]
            for o in range(nonzero):
                value = jnp.zeros((LANES, LANES), F32)
                for s in range(nonzero):
                    live = jnp.logical_and(where[s] == o, block_count[r] > s)
                    scale = jnp.where(live, 1.0, 0.0).astype(F32)
                    value = value + scale * edge_tiles[r, s].astype(F32)
                plan[
                    r // 2,
                    pl.ds((r % 2 + o) * LANES, LANES),
                    pl.ds((r % 2) * LANES, LANES),
                ] = value.T.astype(BF)

    def gated(l, e, k):
        n = GROUP * channels
        for g in range(CHUNK // GROUP):
            start = pl.multiple_of(k * rows + g * n, n)
            for q in range(pairs):
                cols = pl.ds(q * 2 * LANES, 2 * LANES)
                x = xbuf[l, pl.ds(start, (GROUP + DMAX) * channels), cols]
                both = dot(conv_w[l], x) + conv_b[l]
                gate = 0.5 * jnp.tanh(0.5 * both[n:]) + 0.5
                hidden = (jnp.tanh(both[:n]) * gate).astype(BF)
                ext[e, own + 2 * q, pl.ds(start, n), :] = hidden[:, :LANES]
                ext[e, own + 2 * q + 1, pl.ds(start, n), :] = hidden[:, LANES:]

    def diffused(e, k, q):
        at = pl.ds(pl.multiple_of(k * rows, rows), rows)
        source = jnp.concatenate(
            [ext[e, 2 * q + j, at, :] for j in range(2 * reach + 2)], axis=1
        )
        return dot(source, plan[q]).astype(BF)

    def first(e, k):
        at = pl.ds(pl.multiple_of(k * rows, rows), rows)
        for q in range(pairs):
            value = diffused(e, k, q)
            ext[e + 1, own + 2 * q, at, :] = value[:, :LANES]
            ext[e + 1, own + 2 * q + 1, at, :] = value[:, LANES:]

    def pair_of(e, k, q):
        at = pl.ds(pl.multiple_of(k * rows, rows), rows)
        return jnp.concatenate(
            [ext[e, own + 2 * q, at, :], ext[e, own + 2 * q + 1, at, :]], axis=1
        )

    def mixed(l, e, k, q):
        cols = pl.ds(q * 2 * LANES, 2 * LANES)
        second = diffused(e + 1, k, q)
        value = (
            dot(mix_w[l, 0], pair_of(e, k, q))
            + dot(mix_w[l, 1], pair_of(e + 1, k, q))
            + dot(mix_w[l, 2], second)
            + mix_b[l]
        )
        at = pl.ds(pl.multiple_of(k * rows + DMAX * channels, channels), rows)
        return (xbuf[l, at, cols].astype(F32) + value).astype(BF)

    def start_halo(e, k):
        for copy in halo(e, k):
            copy.start()

    def wait_halo(e, k):
        for copy in halo(e, k):
            copy.wait_recv()

    def each(body):
        def step(k, carry):
            body(k)
            return carry

        lax.fori_loop(0, chunks, step, 0)

    def each_half(h, step):
        per = HALF // CHUNK
        lax.fori_loop(h * per, (h + 1) * per, step, 0)

    half_rows = HALF * channels
    square = (half_rows, half_rows)
    i0, i1 = iota(square, 0), iota(square, 1)
    forward = ones_where((i0 % channels) * HALF + i0 // channels == i1)
    for load in loads[halves : halves + 4]:
        load.wait()
    build_conv(0)
    for l in range(LAYERS):
        before = caches[l].astype(F32)
        for t in range(DMAX):
            xbuf[l, pl.ds(t * channels, channels), :] = before[:, t, :].astype(BF)

    def hidden_zero(k, carry):
        gated(0, 0, k)
        start_halo(0, k)
        return carry

    for h in range(halves):
        loads[h].wait()
        piece = series[:, pl.ds(h * HALF, HALF), :].reshape(half_rows, width)
        xbuf[0, pl.ds(DMAX * channels + h * half_rows, half_rows), :] = dot(
            forward, piece
        ).astype(BF)
        if h == 0:
            pl.semaphore_wait(barrier, 2)
        each_half(h, hidden_zero)
    for load in loads[halves + 4 :]:
        load.wait()
    build_plan()
    build_conv(1)
    build_mix(0)

    def first_zero(k):
        wait_halo(0, k)
        first(0, k)
        start_halo(1, k)

    each(first_zero)
    build_mix(1)
    build_skip(0)

    def second_zero(k):
        wait_halo(1, k)
        at = pl.ds(pl.multiple_of(k * rows + DMAX * channels, channels), rows)
        for q in range(pairs):
            xbuf[1, at, pl.ds(q * 2 * LANES, 2 * LANES)] = mixed(0, 0, k, q)
        gated(1, 2, k)
        start_halo(2, k)

    each(second_zero)
    build_skip(1)

    def first_one(k):
        wait_halo(2, k)
        first(2, k)
        start_halo(3, k)

    each(first_one)

    piece = 256
    count = skip_out.shape[0] // piece

    def skip_step(i, carry):
        at = pl.ds(pl.multiple_of(i * piece, piece), piece)
        for q in range(pairs):
            value = dot(skip_w[0, at, :], pair_of(0, chunks - 1, q)) + dot(
                skip_w[1, at, :], pair_of(2, chunks - 1, q)
            )
            skip_out[at, pl.ds(q * 2 * LANES, 2 * LANES)] = value.astype(BF)
        return carry

    lax.fori_loop(0, count, skip_step, 0)
    skip_store = pltpu.make_async_copy(skip_out, skip_hbm, store_sem.at[chunks])
    skip_store.start()

    def store(k):
        at = pl.ds(pl.multiple_of(k * rows, rows), rows)
        return pltpu.make_async_copy(ybuf.at[at, :], next_hbm.at[at, :], store_sem.at[k])

    def second_one(k):
        wait_halo(3, k)
        at = pl.ds(pl.multiple_of(k * rows, rows), rows)
        for q in range(pairs):
            ybuf[at, pl.ds(q * 2 * LANES, 2 * LANES)] = mixed(1, 2, k, q)
        store(k).start()

    each(second_one)

    for e in range(2 * LAYERS):

        def drain(k, e=e):
            for copy in halo(e, k):
                copy.wait_send()

        each(drain)
    each(lambda k: store(k).wait())
    skip_store.wait()


def on_device(
    series,
    caches,
    dilation,
    conv_weight,
    conv_bias,
    mix_weight,
    mix_bias,
    skip_weight,
    block_cols,
    block_count,
    edge_tiles,
):
    channels, steps, width = series.shape
    blocks, nonzero = block_cols.shape
    ring = lax.axis_size("sensor")
    reach = (nonzero - 1) // 2
    skips = skip_weight.shape[1]
    rows = CHUNK * channels
    chunks = steps // CHUNK
    skip_weight = skip_weight.transpose(0, 2, 1)
    hbm = pl.BlockSpec(memory_space=pltpu.HBM)
    operands = (
        series,
        caches,
        dilation,
        conv_weight,
        conv_bias,
        mix_weight,
        mix_bias,
        skip_weight,
        block_cols,
        block_count,
        edge_tiles,
    )
    small = (2, 8, 9)
    places = [
        (pltpu.SMEM if i in small else pltpu.VMEM)(x.shape, x.dtype)
        for i, x in enumerate(operands)
    ]
    loads = len(operands) - 1 + steps // HALF
    following, skip = pl.pallas_call(
        functools.partial(kernel, blocks * ring, ring),
        out_shape=(
            jax.ShapeDtypeStruct((steps * channels, width), BF),
            jax.ShapeDtypeStruct((skips * SKT, width), BF),
        ),
        in_specs=[hbm] * len(operands),
        out_specs=(hbm, hbm),
        scratch_shapes=[
            pltpu.VMEM((skips * SKT, width), BF),
            pltpu.VMEM((2 * LAYERS, blocks + 2 * reach, steps * channels, LANES), BF),
            pltpu.VMEM((LAYERS, (steps + DMAX) * channels, width), BF),
            pltpu.VMEM((steps * channels, width), BF),
            pltpu.VMEM((blocks // 2, (nonzero + 1) * LANES, 2 * LANES), BF),
            pltpu.VMEM((LAYERS, 2 * GROUP * channels, (GROUP + DMAX) * channels), BF),
            pltpu.VMEM((LAYERS, 2 * GROUP * channels, 1), F32),
            pltpu.VMEM((LAYERS, 3, rows, rows), BF),
            pltpu.VMEM((LAYERS, rows, 1), F32),
            pltpu.VMEM((LAYERS, skips * SKT, SKT * channels), BF),
            pltpu.SemaphoreType.DMA((2 * LAYERS, chunks, 2)),
            pltpu.SemaphoreType.DMA((2 * LAYERS, chunks, 2)),
            pltpu.SemaphoreType.DMA((loads,)),
            pltpu.SemaphoreType.DMA((chunks + 1,)),
            *places,
        ],
        compiler_params=pltpu.CompilerParams(
            collective_id=0, has_side_effects=True, vmem_limit_bytes=60 * 2**20
        ),
    )(*operands)
    following = following.reshape(steps, channels, width).transpose(1, 0, 2)
    return following, skip.reshape(skips, SKT, width)


def solution(mesh):
    in_specs = (
        P(None, None, ("groups", "sensor")),
        P(None, None, None, ("groups", "sensor")),
        P(),
        P(),
        P(),
        P(),
        P(),
        P(),
        P(("groups", "sensor"), None),
        P(("groups", "sensor")),
        P(("groups", "sensor"), None, None, None),
    )
    out_specs = (P(None, None, ("groups", "sensor")), P(None, None, ("groups", "sensor")))
    return jax.shard_map(
        on_device, mesh=mesh, in_specs=in_specs, out_specs=out_specs, check_vma=False
    )
```

```python
import functools

import jax
import jax.numpy as jnp
from jax import lax
from jax.experimental import pallas as pl
from jax.experimental.pallas import tpu as pltpu
from jax.sharding import PartitionSpec as P

LAYERS = 2
DMAX = 2
SKT = 8
LANES = 128
CHUNK = 8
GROUP = 4
HALF = 16
BF = jnp.bfloat16
F32 = jnp.float32


def dot(a, b):
    return jnp.dot(a, b, preferred_element_type=F32)


def iota(shape, dim):
    return lax.broadcasted_iota(jnp.int32, shape, dim)


def ones_where(mask):
    return jnp.where(mask, 1.0, 0.0).astype(BF)


def spread(weight, rows, columns):
    o, c = weight.shape
    tall = ones_where(iota((rows, o), 0) % o == iota((rows, o), 1))
    wide = ones_where(iota((c, columns), 1) % c == iota((c, columns), 0))
    return dot(tall, dot(weight, wide).astype(BF))


def column(row_vector, rows):
    c = row_vector.shape[1]
    mask = iota((rows, c), 0) % c == iota((rows, c), 1)
    return jnp.sum(jnp.where(mask, row_vector, 0.0), axis=1, keepdims=True)


def kernel(
    total_blocks,
    ring,
    series_in,
    caches_in,
    dilation_in,
    conv_weight_in,
    conv_bias_in,
    mix_weight_in,
    mix_bias_in,
    skip_weight_in,
    block_cols_in,
    block_count_in,
    edge_tiles_in,
    next_hbm,
    skip_hbm,
    skip_out,
    ext,
    xbuf,
    ybuf,
    plan,
    conv_w,
    conv_b,
    mix_w,
    mix_b,
    skip_w,
    send_sem,
    recv_sem,
    load_sem,
    store_sem,
    series,
    caches,
    dilation,
    conv_weight,
    conv_bias,
    mix_weight,
    mix_bias,
    skip_weight,
    block_cols,
    block_count,
    edge_tiles,
):
    channels, steps, width = series.shape
    blocks = width // LANES
    reach = (block_cols.shape[1] - 1) // 2
    pairs = blocks // 2
    rows = CHUNK * channels
    chunks = steps // CHUNK
    own = reach
    me = lax.axis_index("sensor")
    left, right = lax.rem(me + ring - 1, ring), lax.rem(me + 1, ring)

    halves = steps // HALF
    loads = [
        pltpu.make_async_copy(
            series_in.at[:, pl.ds(h * HALF, HALF), :],
            series.at[:, pl.ds(h * HALF, HALF), :],
            load_sem.at[h],
        )
        for h in range(halves)
    ]
    for source, target in (
        (conv_weight_in, conv_weight),
        (conv_bias_in, conv_bias),
        (dilation_in, dilation),
        (caches_in, caches),
        (edge_tiles_in, edge_tiles),
        (block_cols_in, block_cols),
        (block_count_in, block_count),
        (mix_weight_in, mix_weight),
        (mix_bias_in, mix_bias),
        (skip_weight_in, skip_weight),
    ):
        loads.append(pltpu.make_async_copy(source, target, load_sem.at[len(loads)]))
    for load in loads:
        load.start()

    barrier = pltpu.get_barrier_semaphore()
    for other in (left, right):
        pl.semaphore_signal(
            barrier, inc=1, device_id={"sensor": other}, device_id_type=pl.DeviceIdType.MESH
        )

    def halo(e, k):
        at = pl.ds(pl.multiple_of(k * rows, rows), rows)
        out = []
        for side, (target, source, landing) in enumerate(
            ((right, own + blocks - reach, 0), (left, own, own + blocks))
        ):
            out.append(
                pltpu.make_async_remote_copy(
                    src_ref=ext.at[e, pl.ds(source, reach), at, :],
                    dst_ref=ext.at[e, pl.ds(landing, reach), at, :],
                    send_sem=send_sem.at[e, k, side],
                    recv_sem=recv_sem.at[e, k, side],
                    device_id={"sensor": target},
                    device_id_type=pl.DeviceIdType.MESH,
                )
            )
        return out

    def build_conv(l):
        shape = (GROUP * channels, (GROUP + DMAX) * channels)
        to, ti = iota(shape, 0) // channels, iota(shape, 1) // channels
        late = ti == to + DMAX
        early = ti == to + DMAX - dilation[l]
        n = GROUP * channels
        for g in range(2):
            value = jnp.where(early, spread(conv_weight[l, 2 * g], *shape), 0.0) + jnp.where(
                late, spread(conv_weight[l, 2 * g + 1], *shape), 0.0
            )
            conv_w[l, pl.ds(g * n, n), :] = value.astype(BF)
            conv_b[l, pl.ds(g * n, n), :] = column(conv_bias[l, pl.ds(g, 1), :], n)

    def build_mix(l):
        diagonal = iota((rows, rows), 0) // channels == iota((rows, rows), 1) // channels
        for j in range(3):
            value = jnp.where(diagonal, spread(mix_weight[l, j], rows, rows), 0.0)
            mix_w[l, j] = value.astype(BF)
        mix_b[l] = column(mix_bias[pl.ds(l, 1), :], rows)

    def build_skip(l):
        c, o = skip_weight.shape[1:]
        piece = 512
        wide = ones_where(iota((c, SKT * c), 1) % c == iota((c, SKT * c), 0))
        repeated = dot(skip_weight[l].astype(F32).T.astype(BF), wide).astype(BF)

        def step(i, carry):
            tall = ones_where(
                iota((piece, o), 0) // SKT + i * (piece // SKT) == iota((piece, o), 1)
            )
            mask = iota((piece, SKT * c), 0) % SKT == iota((piece, SKT * c), 1) // c
            at = pl.ds(pl.multiple_of(i * piece, piece), piece)
            skip_w[l, at, :] = jnp.where(mask, dot(tall, repeated), 0.0).astype(BF)
            return carry

        lax.fori_loop(0, o * SKT // piece, step, 0)

    def build_plan():
        plan[...] = jnp.zeros_like(plan)
        nonzero = block_cols.shape[1]
        for r in range(blocks):
            row = me * blocks + r
            where = [
                lax.rem(block_cols[r, s] - row + reach + total_blocks, total_blocks)
                for s in range(nonzero)
            ]
            for o in range(nonzero):
                value = jnp.zeros((LANES, LANES), F32)
                for s in range(nonzero):
                    live = jnp.logical_and(where[s] == o, block_count[r] > s)
                    scale = jnp.where(live, 1.0, 0.0).astype(F32)
                    value = value + scale * edge_tiles[r, s].astype(F32)
                plan[
                    r // 2,
                    pl.ds((r % 2 + o) * LANES, LANES),
                    pl.ds((r % 2) * LANES, LANES),
                ] = value.T.astype(BF)

    def gated(l, e, k):
        n = GROUP * channels
        for g in range(CHUNK // GROUP):
            start = pl.multiple_of(k * rows + g * n, n)
            for q in range(pairs):
                cols = pl.ds(q * 2 * LANES, 2 * LANES)
                x = xbuf[l, pl.ds(start, (GROUP + DMAX) * channels), cols]
                both = dot(conv_w[l], x) + conv_b[l]
                gate = 0.5 * jnp.tanh(0.5 * both[n:]) + 0.5
                hidden = (jnp.tanh(both[:n]) * gate).astype(BF)
                ext[e, own + 2 * q, pl.ds(start, n), :] = hidden[:, :LANES]
                ext[e, own + 2 * q + 1, pl.ds(start, n), :] = hidden[:, LANES:]

    def diffused(e, k, q):
        at = pl.ds(pl.multiple_of(k * rows, rows), rows)
        source = jnp.concatenate(
            [ext[e, 2 * q + j, at, :] for j in range(2 * reach + 2)], axis=1
        )
        return dot(source, plan[q]).astype(BF)

    def first(e, k):
        at = pl.ds(pl.multiple_of(k * rows, rows), rows)
        for q in range(pairs):
            value = diffused(e, k, q)
            ext[e + 1, own + 2 * q, at, :] = value[:, :LANES]
            ext[e + 1, own + 2 * q + 1, at, :] = value[:, LANES:]

    def pair_of(e, k, q):
        at = pl.ds(pl.multiple_of(k * rows, rows), rows)
        return jnp.concatenate(
            [ext[e, own + 2 * q, at, :], ext[e, own + 2 * q + 1, at, :]], axis=1
        )

    def mixed(l, e, k, q):
        cols = pl.ds(q * 2 * LANES, 2 * LANES)
        second = diffused(e + 1, k, q)
        value = (
            dot(mix_w[l, 0], pair_of(e, k, q))
            + dot(mix_w[l, 1], pair_of(e + 1, k, q))
            + dot(mix_w[l, 2], second)
            + mix_b[l]
        )
        at = pl.ds(pl.multiple_of(k * rows + DMAX * channels, channels), rows)
        return (xbuf[l, at, cols].astype(F32) + value).astype(BF)

    def start_halo(e, k):
        for copy in halo(e, k):
            copy.start()

    def wait_halo(e, k):
        for copy in halo(e, k):
            copy.wait_recv()

    def each(body):
        def step(k, carry):
            body(k)
            return carry

        lax.fori_loop(0, chunks, step, 0)

    def each_half(h, step):
        per = HALF // CHUNK
        lax.fori_loop(h * per, (h + 1) * per, step, 0)

    half_rows = HALF * channels
    square = (half_rows, half_rows)
    i0, i1 = iota(square, 0), iota(square, 1)
    forward = ones_where((i0 % channels) * HALF + i0 // channels == i1)
    for load in loads[halves : halves + 4]:
        load.wait()
    build_conv(0)
    for l in range(LAYERS):
        before = caches[l].astype(F32)
        for t in range(DMAX):
            xbuf[l, pl.ds(t * channels, channels), :] = before[:, t, :].astype(BF)

    def hidden_zero(k, carry):
        gated(0, 0, k)
        start_halo(0, k)
        return carry

    for h in range(halves):
        loads[h].wait()
        piece = series[:, pl.ds(h * HALF, HALF), :].reshape(half_rows, width)
        xbuf[0, pl.ds(DMAX * channels + h * half_rows, half_rows), :] = dot(
            forward, piece
        ).astype(BF)
        if h == 0:
            pl.semaphore_wait(barrier, 2)
        each_half(h, hidden_zero)
    for load in loads[halves + 4 :]:
        load.wait()
    build_plan()
    build_conv(1)
    build_mix(0)

    def first_zero(k):
        wait_halo(0, k)
        first(0, k)
        start_halo(1, k)

    each(first_zero)
    build_mix(1)
    build_skip(0)

    def second_zero(k):
        wait_halo(1, k)
        at = pl.ds(pl.multiple_of(k * rows + DMAX * channels, channels), rows)
        for q in range(pairs):
            xbuf[1, at, pl.ds(q * 2 * LANES, 2 * LANES)] = mixed(0, 0, k, q)
        gated(1, 2, k)
        start_halo(2, k)

    each(second_zero)
    build_skip(1)

    def first_one(k):
        wait_halo(2, k)
        first(2, k)
        start_halo(3, k)

    each(first_one)

    piece = 256
    count = skip_out.shape[0] // piece

    def skip_step(i, carry):
        at = pl.ds(pl.multiple_of(i * piece, piece), piece)
        for q in range(pairs):
            value = dot(skip_w[0, at, :], pair_of(0, chunks - 1, q)) + dot(
                skip_w[1, at, :], pair_of(2, chunks - 1, q)
            )
            skip_out[at, pl.ds(q * 2 * LANES, 2 * LANES)] = value.astype(BF)
        return carry

    lax.fori_loop(0, count, skip_step, 0)
    skip_store = pltpu.make_async_copy(skip_out, skip_hbm, store_sem.at[chunks])
    skip_store.start()

    def store(k):
        at = pl.ds(pl.multiple_of(k * rows, rows), rows)
        return pltpu.make_async_copy(ybuf.at[at, :], next_hbm.at[at, :], store_sem.at[k])

    def second_one(k):
        wait_halo(3, k)
        at = pl.ds(pl.multiple_of(k * rows, rows), rows)
        for q in range(pairs):
            ybuf[at, pl.ds(q * 2 * LANES, 2 * LANES)] = mixed(1, 2, k, q)
        store(k).start()

    each(second_one)

    for e in range(2 * LAYERS):

        def drain(k, e=e):
            for copy in halo(e, k):
                copy.wait_send()

        each(drain)
    each(lambda k: store(k).wait())
    skip_store.wait()


def finish(y_in, skip_in, next_hbm, skip_hbm, y, out, skip, load_sem, store_sem):
    channels, _, width = out.shape
    rows = HALF * channels
    halves = y.shape[0] // rows
    part = skip.shape[0] // halves
    y_at = [pl.ds(h * rows, rows) for h in range(halves)]
    skip_at = [pl.ds(h * part, part) for h in range(halves)]
    loads = [
        pltpu.make_async_copy(y_in.at[at, :], y.at[at, :], load_sem.at[h])
        for h, at in enumerate(y_at)
    ] + [
        pltpu.make_async_copy(skip_in.at[at, :], skip.at[at, :], load_sem.at[halves + h])
        for h, at in enumerate(skip_at)
    ]
    for load in loads:
        load.start()
    i0, i1 = iota((rows, rows), 0), iota((rows, rows), 1)
    backward = ones_where((i0 % HALF) * channels + i0 // HALF == i1)
    stores = []
    for h in range(halves):
        loads[h].wait()
        value = dot(backward, y[y_at[h], :]).astype(BF)
        times = pl.ds(h * HALF, HALF)
        out[:, times, :] = value.reshape(channels, HALF, width)
        stores.append(
            pltpu.make_async_copy(out.at[:, times, :], next_hbm.at[:, times, :], store_sem.at[h])
        )
        stores[-1].start()
    for h, at in enumerate(skip_at):
        loads[halves + h].wait()
        stores.append(
            pltpu.make_async_copy(skip.at[at, :], skip_hbm.at[at, :], store_sem.at[halves + h])
        )
        stores[-1].start()
    for store in stores:
        store.wait()


def on_device(
    series,
    caches,
    dilation,
    conv_weight,
    conv_bias,
    mix_weight,
    mix_bias,
    skip_weight,
    block_cols,
    block_count,
    edge_tiles,
):
    channels, steps, width = series.shape
    blocks, nonzero = block_cols.shape
    ring = lax.axis_size("sensor")
    reach = (nonzero - 1) // 2
    skips = skip_weight.shape[1]
    rows = CHUNK * channels
    chunks = steps // CHUNK
    skip_weight = skip_weight.transpose(0, 2, 1)
    hbm = pl.BlockSpec(memory_space=pltpu.HBM)
    operands = (
        series,
        caches,
        dilation,
        conv_weight,
        conv_bias,
        mix_weight,
        mix_bias,
        skip_weight,
        block_cols,
        block_count,
        edge_tiles,
    )
    small = (2, 8, 9)
    places = [
        (pltpu.SMEM if i in small else pltpu.VMEM)(x.shape, x.dtype)
        for i, x in enumerate(operands)
    ]
    loads = len(operands) - 1 + steps // HALF
    following, skip = pl.pallas_call(
        functools.partial(kernel, blocks * ring, ring),
        out_shape=(
            jax.ShapeDtypeStruct((steps * channels, width), BF),
            jax.ShapeDtypeStruct((skips * SKT, width), BF),
        ),
        in_specs=[hbm] * len(operands),
        out_specs=(hbm, hbm),
        scratch_shapes=[
            pltpu.VMEM((skips * SKT, width), BF),
            pltpu.VMEM((2 * LAYERS, blocks + 2 * reach, steps * channels, LANES), BF),
            pltpu.VMEM((LAYERS, (steps + DMAX) * channels, width), BF),
            pltpu.VMEM((steps * channels, width), BF),
            pltpu.VMEM((blocks // 2, (nonzero + 1) * LANES, 2 * LANES), BF),
            pltpu.VMEM((LAYERS, 2 * GROUP * channels, (GROUP + DMAX) * channels), BF),
            pltpu.VMEM((LAYERS, 2 * GROUP * channels, 1), F32),
            pltpu.VMEM((LAYERS, 3, rows, rows), BF),
            pltpu.VMEM((LAYERS, rows, 1), F32),
            pltpu.VMEM((LAYERS, skips * SKT, SKT * channels), BF),
            pltpu.SemaphoreType.DMA((2 * LAYERS, chunks, 2)),
            pltpu.SemaphoreType.DMA((2 * LAYERS, chunks, 2)),
            pltpu.SemaphoreType.DMA((loads,)),
            pltpu.SemaphoreType.DMA((chunks + 1,)),
            *places,
        ],
        compiler_params=pltpu.CompilerParams(
            collective_id=0, has_side_effects=True, vmem_limit_bytes=60 * 2**20
        ),
    )(*operands)
    halves = steps // HALF
    following, skip = pl.pallas_call(
        finish,
        out_shape=(
            jax.ShapeDtypeStruct((channels, steps, width), BF),
            jax.ShapeDtypeStruct(skip.shape, BF),
        ),
        in_specs=[hbm, hbm],
        out_specs=(hbm, hbm),
        scratch_shapes=[
            pltpu.VMEM(following.shape, BF),
            pltpu.VMEM((channels, steps, width), BF),
            pltpu.VMEM(skip.shape, BF),
            pltpu.SemaphoreType.DMA((2 * halves,)),
            pltpu.SemaphoreType.DMA((2 * halves,)),
        ],
        compiler_params=pltpu.CompilerParams(vmem_limit_bytes=60 * 2**20),
    )(following, skip)
    return following, skip.reshape(skips, SKT, width)


def solution(mesh):
    in_specs = (
        P(None, None, ("groups", "sensor")),
        P(None, None, None, ("groups", "sensor")),
        P(),
        P(),
        P(),
        P(),
        P(),
        P(),
        P(("groups", "sensor"), None),
        P(("groups", "sensor")),
        P(("groups", "sensor"), None, None, None),
    )
    out_specs = (P(None, None, ("groups", "sensor")), P(None, None, ("groups", "sensor")))
    return jax.shard_map(
        on_device, mesh=mesh, in_specs=in_specs, out_specs=out_specs, check_vma=False
    )
```

```python
import functools

import jax
import jax.numpy as jnp
from jax import lax
from jax.experimental import pallas as pl
from jax.experimental.pallas import tpu as pltpu
from jax.sharding import PartitionSpec as P

LAYERS = 2
DMAX = 2
SKT = 8
LANES = 128
CHUNK = 4
GROUP = 4
HALF = 16
BF = jnp.bfloat16
F32 = jnp.float32


def dot(a, b):
    return jnp.dot(a, b, preferred_element_type=F32)


def iota(shape, dim):
    return lax.broadcasted_iota(jnp.int32, shape, dim)


def ones_where(mask):
    return jnp.where(mask, 1.0, 0.0).astype(BF)


def spread(weight, rows, columns):
    o, c = weight.shape
    tall = ones_where(iota((rows, o), 0) % o == iota((rows, o), 1))
    wide = ones_where(iota((c, columns), 1) % c == iota((c, columns), 0))
    return dot(tall, dot(weight, wide).astype(BF))


def column(row_vector, rows):
    c = row_vector.shape[1]
    mask = iota((rows, c), 0) % c == iota((rows, c), 1)
    return jnp.sum(jnp.where(mask, row_vector, 0.0), axis=1, keepdims=True)


def kernel(
    total_blocks,
    ring,
    series_in,
    caches_in,
    dilation_in,
    conv_weight_in,
    conv_bias_in,
    mix_weight_in,
    mix_bias_in,
    skip_weight_in,
    block_cols_in,
    block_count_in,
    edge_tiles_in,
    next_hbm,
    skip_hbm,
    skip_out,
    ext,
    xbuf,
    ybuf,
    plan,
    conv_w,
    conv_b,
    mix_w,
    mix_b,
    skip_w,
    send_sem,
    recv_sem,
    load_sem,
    store_sem,
    series,
    caches,
    dilation,
    conv_weight,
    conv_bias,
    mix_weight,
    mix_bias,
    skip_weight,
    block_cols,
    block_count,
    edge_tiles,
):
    channels, steps, width = series.shape
    blocks = width // LANES
    reach = (block_cols.shape[1] - 1) // 2
    pairs = blocks // 2
    rows = CHUNK * channels
    chunks = steps // CHUNK
    own = reach
    me = lax.axis_index("sensor")
    left, right = lax.rem(me + ring - 1, ring), lax.rem(me + 1, ring)

    halves = steps // HALF
    loads = [
        pltpu.make_async_copy(
            series_in.at[:, pl.ds(h * HALF, HALF), :],
            series.at[:, pl.ds(h * HALF, HALF), :],
            load_sem.at[h],
        )
        for h in range(halves)
    ]
    for source, target in (
        (conv_weight_in, conv_weight),
        (conv_bias_in, conv_bias),
        (dilation_in, dilation),
        (caches_in, caches),
        (edge_tiles_in, edge_tiles),
        (block_cols_in, block_cols),
        (block_count_in, block_count),
        (mix_weight_in, mix_weight),
        (mix_bias_in, mix_bias),
        (skip_weight_in, skip_weight),
    ):
        loads.append(pltpu.make_async_copy(source, target, load_sem.at[len(loads)]))
    for load in loads:
        load.start()

    barrier = pltpu.get_barrier_semaphore()
    for other in (left, right):
        pl.semaphore_signal(
            barrier, inc=1, device_id={"sensor": other}, device_id_type=pl.DeviceIdType.MESH
        )

    def halo(e, k):
        at = pl.ds(pl.multiple_of(k * rows, rows), rows)
        out = []
        for side, (target, source, landing) in enumerate(
            ((right, own + blocks - reach, 0), (left, own, own + blocks))
        ):
            out.append(
                pltpu.make_async_remote_copy(
                    src_ref=ext.at[e, pl.ds(source, reach), at, :],
                    dst_ref=ext.at[e, pl.ds(landing, reach), at, :],
                    send_sem=send_sem.at[e, k, side],
                    recv_sem=recv_sem.at[e, k, side],
                    device_id={"sensor": target},
                    device_id_type=pl.DeviceIdType.MESH,
                )
            )
        return out

    def build_conv(l):
        shape = (GROUP * channels, (GROUP + DMAX) * channels)
        to, ti = iota(shape, 0) // channels, iota(shape, 1) // channels
        late = ti == to + DMAX
        early = ti == to + DMAX - dilation[l]
        n = GROUP * channels
        for g in range(2):
            value = jnp.where(early, spread(conv_weight[l, 2 * g], *shape), 0.0) + jnp.where(
                late, spread(conv_weight[l, 2 * g + 1], *shape), 0.0
            )
            conv_w[l, pl.ds(g * n, n), :] = value.astype(BF)
            conv_b[l, pl.ds(g * n, n), :] = column(conv_bias[l, pl.ds(g, 1), :], n)

    def build_mix(l):
        diagonal = iota((rows, rows), 0) // channels == iota((rows, rows), 1) // channels
        for j in range(3):
            value = jnp.where(diagonal, spread(mix_weight[l, j], rows, rows), 0.0)
            mix_w[l, j] = value.astype(BF)
        mix_b[l] = column(mix_bias[pl.ds(l, 1), :], rows)

    def build_skip(l):
        c, o = skip_weight.shape[1:]
        piece = 512
        wide = ones_where(iota((c, SKT * c), 1) % c == iota((c, SKT * c), 0))
        repeated = dot(skip_weight[l].astype(F32).T.astype(BF), wide).astype(BF)

        def step(i, carry):
            tall = ones_where(
                iota((piece, o), 0) // SKT + i * (piece // SKT) == iota((piece, o), 1)
            )
            mask = iota((piece, SKT * c), 0) % SKT == iota((piece, SKT * c), 1) // c
            at = pl.ds(pl.multiple_of(i * piece, piece), piece)
            skip_w[l, at, :] = jnp.where(mask, dot(tall, repeated), 0.0).astype(BF)
            return carry

        lax.fori_loop(0, o * SKT // piece, step, 0)

    def build_plan():
        plan[...] = jnp.zeros_like(plan)
        nonzero = block_cols.shape[1]
        for r in range(blocks):
            row = me * blocks + r
            where = [
                lax.rem(block_cols[r, s] - row + reach + total_blocks, total_blocks)
                for s in range(nonzero)
            ]
            for o in range(nonzero):
                value = jnp.zeros((LANES, LANES), F32)
                for s in range(nonzero):
                    live = jnp.logical_and(where[s] == o, block_count[r] > s)
                    scale = jnp.where(live, 1.0, 0.0).astype(F32)
                    value = value + scale * edge_tiles[r, s].astype(F32)
                plan[
                    r // 2,
                    pl.ds((r % 2 + o) * LANES, LANES),
                    pl.ds((r % 2) * LANES, LANES),
                ] = value.T.astype(BF)

    def gated(l, e, k):
        n = GROUP * channels
        for g in range(CHUNK // GROUP):
            start = pl.multiple_of(k * rows + g * n, n)
            for q in range(pairs):
                cols = pl.ds(q * 2 * LANES, 2 * LANES)
                x = xbuf[l, pl.ds(start, (GROUP + DMAX) * channels), cols]
                both = dot(conv_w[l], x) + conv_b[l]
                gate = 0.5 * jnp.tanh(0.5 * both[n:]) + 0.5
                hidden = (jnp.tanh(both[:n]) * gate).astype(BF)
                ext[e, own + 2 * q, pl.ds(start, n), :] = hidden[:, :LANES]
                ext[e, own + 2 * q + 1, pl.ds(start, n), :] = hidden[:, LANES:]

    def diffused(e, k, q):
        at = pl.ds(pl.multiple_of(k * rows, rows), rows)
        source = jnp.concatenate(
            [ext[e, 2 * q + j, at, :] for j in range(2 * reach + 2)], axis=1
        )
        return dot(source, plan[q]).astype(BF)

    def first(e, k):
        at = pl.ds(pl.multiple_of(k * rows, rows), rows)
        for q in range(pairs):
            value = diffused(e, k, q)
            ext[e + 1, own + 2 * q, at, :] = value[:, :LANES]
            ext[e + 1, own + 2 * q + 1, at, :] = value[:, LANES:]

    def pair_of(e, k, q):
        at = pl.ds(pl.multiple_of(k * rows, rows), rows)
        return jnp.concatenate(
            [ext[e, own + 2 * q, at, :], ext[e, own + 2 * q + 1, at, :]], axis=1
        )

    def tail_of(e, q):
        at = pl.ds((steps - SKT) * channels, SKT * channels)
        return jnp.concatenate(
            [ext[e, own + 2 * q, at, :], ext[e, own + 2 * q + 1, at, :]], axis=1
        )

    def mixed(l, e, k, q):
        cols = pl.ds(q * 2 * LANES, 2 * LANES)
        second = diffused(e + 1, k, q)
        value = (
            dot(mix_w[l, 0], pair_of(e, k, q))
            + dot(mix_w[l, 1], pair_of(e + 1, k, q))
            + dot(mix_w[l, 2], second)
            + mix_b[l]
        )
        at = pl.ds(pl.multiple_of(k * rows + DMAX * channels, channels), rows)
        return (xbuf[l, at, cols].astype(F32) + value).astype(BF)

    def start_halo(e, k):
        for copy in halo(e, k):
            copy.start()

    def wait_halo(e, k):
        for copy in halo(e, k):
            copy.wait_recv()

    def each(body):
        def step(k, carry):
            body(k)
            return carry

        lax.fori_loop(0, chunks, step, 0)

    def each_half(h, step):
        per = HALF // CHUNK
        lax.fori_loop(h * per, (h + 1) * per, step, 0)

    half_rows = HALF * channels
    square = (half_rows, half_rows)
    i0, i1 = iota(square, 0), iota(square, 1)
    forward = ones_where((i0 % channels) * HALF + i0 // channels == i1)
    for load in loads[halves : halves + 4]:
        load.wait()
    build_conv(0)
    for l in range(LAYERS):
        before = caches[l].astype(F32)
        for t in range(DMAX):
            xbuf[l, pl.ds(t * channels, channels), :] = before[:, t, :].astype(BF)

    def hidden_zero(k, carry):
        gated(0, 0, k)
        start_halo(0, k)
        return carry

    for h in range(halves):
        loads[h].wait()
        piece = series[:, pl.ds(h * HALF, HALF), :].reshape(half_rows, width)
        xbuf[0, pl.ds(DMAX * channels + h * half_rows, half_rows), :] = dot(
            forward, piece
        ).astype(BF)
        if h == 0:
            pl.semaphore_wait(barrier, 2)
        each_half(h, hidden_zero)
    for load in loads[halves + 4 :]:
        load.wait()
    build_plan()
    build_conv(1)
    build_mix(0)

    def first_zero(k):
        wait_halo(0, k)
        first(0, k)
        start_halo(1, k)

    each(first_zero)
    build_mix(1)
    build_skip(0)

    def second_zero(k):
        wait_halo(1, k)
        at = pl.ds(pl.multiple_of(k * rows + DMAX * channels, channels), rows)
        for q in range(pairs):
            xbuf[1, at, pl.ds(q * 2 * LANES, 2 * LANES)] = mixed(0, 0, k, q)
        gated(1, 2, k)
        start_halo(2, k)

    each(second_zero)
    build_skip(1)

    def first_one(k):
        wait_halo(2, k)
        first(2, k)
        start_halo(3, k)

    each(first_one)

    piece = 256
    count = skip_out.shape[0] // piece

    def skip_step(i, carry):
        at = pl.ds(pl.multiple_of(i * piece, piece), piece)
        for q in range(pairs):
            value = dot(skip_w[0, at, :], tail_of(0, q)) + dot(skip_w[1, at, :], tail_of(2, q))
            skip_out[at, pl.ds(q * 2 * LANES, 2 * LANES)] = value.astype(BF)
        return carry

    lax.fori_loop(0, count, skip_step, 0)
    skip_store = pltpu.make_async_copy(skip_out, skip_hbm, store_sem.at[chunks])
    skip_store.start()

    def store(k):
        at = pl.ds(pl.multiple_of(k * rows, rows), rows)
        return pltpu.make_async_copy(ybuf.at[at, :], next_hbm.at[at, :], store_sem.at[k])

    def second_one(k):
        wait_halo(3, k)
        at = pl.ds(pl.multiple_of(k * rows, rows), rows)
        for q in range(pairs):
            ybuf[at, pl.ds(q * 2 * LANES, 2 * LANES)] = mixed(1, 2, k, q)
        store(k).start()

    each(second_one)

    for e in range(2 * LAYERS):

        def drain(k, e=e):
            for copy in halo(e, k):
                copy.wait_send()

        each(drain)
    each(lambda k: store(k).wait())
    skip_store.wait()


def finish(y_in, skip_in, next_hbm, skip_hbm, y, out, skip, load_sem, store_sem):
    channels, _, width = out.shape
    rows = HALF * channels
    halves = y.shape[0] // rows
    part = skip.shape[0] // halves
    y_at = [pl.ds(h * rows, rows) for h in range(halves)]
    skip_at = [pl.ds(h * part, part) for h in range(halves)]
    loads = [
        pltpu.make_async_copy(y_in.at[at, :], y.at[at, :], load_sem.at[h])
        for h, at in enumerate(y_at)
    ] + [
        pltpu.make_async_copy(skip_in.at[at, :], skip.at[at, :], load_sem.at[halves + h])
        for h, at in enumerate(skip_at)
    ]
    for load in loads:
        load.start()
    i0, i1 = iota((rows, rows), 0), iota((rows, rows), 1)
    backward = ones_where((i0 % HALF) * channels + i0 // HALF == i1)
    stores = []
    for h in range(halves):
        loads[h].wait()
        value = dot(backward, y[y_at[h], :]).astype(BF)
        times = pl.ds(h * HALF, HALF)
        out[:, times, :] = value.reshape(channels, HALF, width)
        stores.append(
            pltpu.make_async_copy(out.at[:, times, :], next_hbm.at[:, times, :], store_sem.at[h])
        )
        stores[-1].start()
    for h, at in enumerate(skip_at):
        loads[halves + h].wait()
        stores.append(
            pltpu.make_async_copy(skip.at[at, :], skip_hbm.at[at, :], store_sem.at[halves + h])
        )
        stores[-1].start()
    for store in stores:
        store.wait()


def on_device(
    series,
    caches,
    dilation,
    conv_weight,
    conv_bias,
    mix_weight,
    mix_bias,
    skip_weight,
    block_cols,
    block_count,
    edge_tiles,
):
    channels, steps, width = series.shape
    blocks, nonzero = block_cols.shape
    ring = lax.axis_size("sensor")
    reach = (nonzero - 1) // 2
    skips = skip_weight.shape[1]
    rows = CHUNK * channels
    chunks = steps // CHUNK
    skip_weight = skip_weight.transpose(0, 2, 1)
    hbm = pl.BlockSpec(memory_space=pltpu.HBM)
    operands = (
        series,
        caches,
        dilation,
        conv_weight,
        conv_bias,
        mix_weight,
        mix_bias,
        skip_weight,
        block_cols,
        block_count,
        edge_tiles,
    )
    small = (2, 8, 9)
    places = [
        (pltpu.SMEM if i in small else pltpu.VMEM)(x.shape, x.dtype)
        for i, x in enumerate(operands)
    ]
    loads = len(operands) - 1 + steps // HALF
    following, skip = pl.pallas_call(
        functools.partial(kernel, blocks * ring, ring),
        out_shape=(
            jax.ShapeDtypeStruct((steps * channels, width), BF),
            jax.ShapeDtypeStruct((skips * SKT, width), BF),
        ),
        in_specs=[hbm] * len(operands),
        out_specs=(hbm, hbm),
        scratch_shapes=[
            pltpu.VMEM((skips * SKT, width), BF),
            pltpu.VMEM((2 * LAYERS, blocks + 2 * reach, steps * channels, LANES), BF),
            pltpu.VMEM((LAYERS, (steps + DMAX) * channels, width), BF),
            pltpu.VMEM((steps * channels, width), BF),
            pltpu.VMEM((blocks // 2, (nonzero + 1) * LANES, 2 * LANES), BF),
            pltpu.VMEM((LAYERS, 2 * GROUP * channels, (GROUP + DMAX) * channels), BF),
            pltpu.VMEM((LAYERS, 2 * GROUP * channels, 1), F32),
            pltpu.VMEM((LAYERS, 3, rows, rows), BF),
            pltpu.VMEM((LAYERS, rows, 1), F32),
            pltpu.VMEM((LAYERS, skips * SKT, SKT * channels), BF),
            pltpu.SemaphoreType.DMA((2 * LAYERS, chunks, 2)),
            pltpu.SemaphoreType.DMA((2 * LAYERS, chunks, 2)),
            pltpu.SemaphoreType.DMA((loads,)),
            pltpu.SemaphoreType.DMA((chunks + 1,)),
            *places,
        ],
        compiler_params=pltpu.CompilerParams(
            collective_id=0, has_side_effects=True, vmem_limit_bytes=60 * 2**20
        ),
    )(*operands)
    halves = steps // HALF
    following, skip = pl.pallas_call(
        finish,
        out_shape=(
            jax.ShapeDtypeStruct((channels, steps, width), BF),
            jax.ShapeDtypeStruct(skip.shape, BF),
        ),
        in_specs=[hbm, hbm],
        out_specs=(hbm, hbm),
        scratch_shapes=[
            pltpu.VMEM(following.shape, BF),
            pltpu.VMEM((channels, steps, width), BF),
            pltpu.VMEM(skip.shape, BF),
            pltpu.SemaphoreType.DMA((2 * halves,)),
            pltpu.SemaphoreType.DMA((2 * halves,)),
        ],
        compiler_params=pltpu.CompilerParams(vmem_limit_bytes=60 * 2**20),
    )(following, skip)
    return following, skip.reshape(skips, SKT, width)


def solution(mesh):
    in_specs = (
        P(None, None, ("groups", "sensor")),
        P(None, None, None, ("groups", "sensor")),
        P(),
        P(),
        P(),
        P(),
        P(),
        P(),
        P(("groups", "sensor"), None),
        P(("groups", "sensor")),
        P(("groups", "sensor"), None, None, None),
    )
    out_specs = (P(None, None, ("groups", "sensor")), P(None, None, ("groups", "sensor")))
    return jax.shard_map(
        on_device, mesh=mesh, in_specs=in_specs, out_specs=out_specs, check_vma=False
    )
```
